32 devices in a mesh: gx: 2 (over x), gy: 4 (over z), cyc: 4 (over y, core).
Axes of the slice: x: 2, y: 2, z: 4, core: 2. Of those that a mesh axis runs over, the one named last changes fastest.
Arguments:
- displacement: bfloat16 [2, 48, 512, 1024], P(None, 'gx', 'gy', 'cyc'), may hold values from -6 to 6
Outputs:
- basis: float32 [2, 48, 512, 128], P(None, 'gx', 'gy', 'cyc')
The draws below stay inside these ranges and needn't reach their ends.
All inputs are finite; a program needn't handle non-finite values.
Results may differ from the reference program's by a relative error of at most 0.0003.
Values may be sent and summed in bfloat16 or wider, within the bound.
A program may use at most 128 MiB of HBM per device.

```python
import jax
import jax.numpy as jnp
from jax import lax

SNAP_DEV = 256
RANK = 128
POWER = 3
NX = 48
NY = 512
SNAPS = 1024
N_CYC = 4


def steps_of(own_key, extent, cuts, low, high):
    level = 1.0
    for position, shards_of in cuts:
        heights = jax.random.uniform(jax.random.fold_in(jax.random.fold_in(own_key, 6), position), (shards_of,), jnp.float32, low / len(cuts), high / len(cuts))
        level = level * jnp.repeat(jnp.exp(heights), extent[position] // shards_of).reshape((-1,) + (1,) * (len(extent) - 1 - position))
    return level


def noise(stream_key, dims, scale, bound, shards=(), held_as=jnp.bfloat16):
    array = scale * jax.random.normal(stream_key, dims, jnp.float32)
    if shards:
        array = array * steps_of(stream_key, dims, shards, -0.22, 0.18)
    return jnp.clip(array, -bound, bound).astype(held_as)


def setup_inputs(seed: int = 0) -> dict:
    arg_keys = jax.random.split(jax.random.key(seed), 2)
    displacement = noise(arg_keys[0], (2, NX, NY, SNAPS), 1.0, 6.0, ((1, 2), (2, 4), (3, 4)))
    return dict(displacement=displacement)


def strain_rows(padded):
    field = padded.astype(jnp.float32)
    along_x = (field[:, 2:, 1:-1] - field[:, :-2, 1:-1]) * 0.5
    along_y = (field[:, 1:-1, 2:] - field[:, 1:-1, :-2]) * 0.5
    strain_xx = along_x[0]
    strain_yy = along_y[1]
    strain_xy = 0.5 * (along_x[1] + along_y[0])
    first = strain_xx + strain_yy
    second = strain_xx * strain_yy - strain_xy * strain_xy
    return jnp.stack([first, second]).reshape(-1, padded.shape[-1])

def gram_of(joined):
    return lax.dot_general(joined.astype(jnp.float32), joined.astype(jnp.float32), (((0,), (0,)), ((), ())), precision=lax.Precision.HIGHEST, preferred_element_type=jnp.float32)

def finish(joined, gram):
    width = gram.shape[0]
    normed = gram / (jnp.trace(gram) / width + 1e-06)
    vectors = (jnp.arange(width)[:, None] % RANK == jnp.arange(RANK)[None, :]).astype(jnp.float32)
    for step in range(POWER):
        moved = jnp.dot(normed.astype(jnp.float32), vectors.astype(jnp.float32), precision=lax.Precision.HIGHEST, preferred_element_type=jnp.float32)
        lower = jnp.linalg.cholesky(gram_of(moved))
        vectors = lax.linalg.triangular_solve(lower, moved, left_side=False, lower=True, transpose_a=True)
    return jnp.dot(joined.astype(jnp.float32), vectors.astype(jnp.float32), precision=lax.Precision.HIGHEST, preferred_element_type=jnp.float32)

def truncate(joined):
    return finish(joined, gram_of(joined))

def reference(displacement):
    pieces = []
    for group in range(N_CYC):
        block = displacement[..., group * SNAP_DEV:(group + 1) * SNAP_DEV]
        padded = jnp.pad(block, ((0, 0), (1, 1), (1, 1), (0, 0)))
        pieces.append(truncate(strain_rows(padded)))
    pair_low = truncate(jnp.concatenate([pieces[0], pieces[1]], axis=1))
    pair_high = truncate(jnp.concatenate([pieces[2], pieces[3]], axis=1))
    basis = truncate(jnp.concatenate([pair_low, pair_high], axis=1))
    return basis.reshape(2, NX, NY, RANK)
```

```python
import functools

import jax
import jax.numpy as jnp
from jax import lax
from jax.experimental import pallas as pl
from jax.experimental.pallas import tpu as pltpu
from jax.sharding import PartitionSpec as P

RANK = 128
POWER = 3
PANEL = 16
MESH = pl.DeviceIdType.MESH
HIGH = lax.Precision.HIGH
HIGHEST = lax.Precision.HIGHEST
VMEM_LIMIT = 48 * 1024 * 1024


def neighbours(block, axis, dim):
    count = lax.axis_size(axis)
    forward = [(i, i + 1) for i in range(count - 1)]
    backward = [(target, source) for source, target in forward]
    size = block.shape[dim]
    low = lax.ppermute(lax.slice_in_dim(block, size - 1, size, axis=dim), axis, forward)
    high = lax.ppermute(lax.slice_in_dim(block, 0, 1, axis=dim), axis, backward)
    return low, high


def exchanged(value, mask):
    pairs = [(source, source ^ mask) for source in range(lax.axis_size("cyc"))]
    return lax.ppermute(value, "cyc", pairs)


def contract(left, right, dims, precision=None):
    return lax.dot_general(
        left, right, (dims, ((), ())), precision=precision, preferred_element_type=jnp.float32
    )


def upper_blocks(gram_ref, full):
    gram_ref[0:RANK] = full[:RANK, :RANK]
    gram_ref[RANK : 2 * RANK] = full[:RANK, RANK:]
    gram_ref[2 * RANK : 3 * RANK] = full[RANK:, RANK:]
    if gram_ref.shape[0] > 3 * RANK:
        gram_ref[3 * RANK :] = jnp.zeros((gram_ref.shape[0] - 3 * RANK, RANK), jnp.float32)


def split(value):
    high = value.astype(jnp.bfloat16)
    return high, (value - high.astype(jnp.float32)).astype(jnp.bfloat16)


def add_gram(main, cross, value):
    high, low = split(value)
    main[...] += contract(high, high, ((0,), (0,)))
    cross[...] += contract(high, low, ((0,), (0,)))


def strain_kernel(u_ref, xlo_ref, xhi_ref, ylo_ref, yhi_ref, f_ref, gram_ref, main, cross):
    i = pl.program_id(0)
    rows = pl.num_programs(0)
    cols = u_ref.shape[2]

    @pl.when(i == 0)
    def _():
        main[...] = jnp.zeros_like(main)
        cross[...] = jnp.zeros_like(cross)

    node = lax.broadcasted_iota(jnp.int32, (cols, u_ref.shape[3]), 0)

    def dx(part):
        before = u_ref[part, jnp.maximum(i - 1, 0)].astype(jnp.float32)
        after = u_ref[part, jnp.minimum(i + 1, rows - 1)].astype(jnp.float32)
        before = jnp.where(i == 0, xlo_ref[part, 0].astype(jnp.float32), before)
        after = jnp.where(i == rows - 1, xhi_ref[part, 0].astype(jnp.float32), after)
        return (after - before) * 0.5

    def dy(part):
        here = u_ref[part, i].astype(jnp.float32)
        before = pltpu.roll(here, 1, 0)
        after = pltpu.roll(here, cols - 1, 0)
        before = jnp.where(node == 0, ylo_ref[part, i].astype(jnp.float32), before)
        after = jnp.where(node == cols - 1, yhi_ref[part, i].astype(jnp.float32), after)
        return (after - before) * 0.5

    exx = dx(0)
    eyy = dy(1)
    exy = (dx(1) + dy(0)) * 0.5
    first = exx + eyy
    second = exx * eyy - exy * exy
    f_ref[0, 0] = first
    f_ref[1, 0] = second
    add_gram(main, cross, first)
    add_gram(main, cross, second)

    @pl.when(i == rows - 1)
    def _():
        upper_blocks(gram_ref, main[...] + cross[...] + cross[...].T)


def strain(u, halo, padded):
    parts, rows, cols, width = u.shape
    whole = [pl.BlockSpec(a.shape, lambda i: (0, 0, 0, 0)) for a in (u, *halo)]
    return pl.pallas_call(
        strain_kernel,
        grid=(rows,),
        in_specs=whole,
        out_specs=[
            pl.BlockSpec((parts, 1, cols, width), lambda i: (0, i, 0, 0)),
            pl.BlockSpec((padded, RANK), lambda i: (0, 0)),
        ],
        out_shape=[
            jax.ShapeDtypeStruct((parts, rows, cols, width), jnp.float32),
            jax.ShapeDtypeStruct((padded, RANK), jnp.float32),
        ],
        scratch_shapes=[pltpu.VMEM((width, width), jnp.float32)] * 2,
        compiler_params=pltpu.CompilerParams(vmem_limit_bytes=VMEM_LIMIT),
    )(u, *halo)


def gram_kernel(left_ref, right_ref, gram_ref, main, cross):
    step = pl.program_id(0)

    @pl.when(step == 0)
    def _():
        main[...] = jnp.zeros_like(main)
        cross[...] = jnp.zeros_like(cross)

    add_gram(main, cross, jnp.concatenate([left_ref[...], right_ref[...]], axis=1))

    @pl.when(step == pl.num_programs(0) - 1)
    def _():
        upper_blocks(gram_ref, main[...] + cross[...] + cross[...].T)


def gram_of(left, right, padded):
    rows = left.shape[0]
    tile = 512 if rows % 512 == 0 else rows
    spec = pl.BlockSpec((tile, RANK), lambda i: (i, 0))
    return pl.pallas_call(
        gram_kernel,
        grid=(rows // tile,),
        in_specs=[spec, spec],
        out_specs=pl.BlockSpec((padded, RANK), lambda i: (0, 0)),
        out_shape=jax.ShapeDtypeStruct((padded, RANK), jnp.float32),
        scratch_shapes=[pltpu.VMEM((2 * RANK, 2 * RANK), jnp.float32)] * 2,
        compiler_params=pltpu.CompilerParams(vmem_limit_bytes=VMEM_LIMIT),
    )(left, right)


def sum_kernel(sizes, x_ref, o_ref, held, send_a, recv_a, send_b, recv_b):
    n_x, n_y, near = sizes
    n = n_x * n_y * near
    chunk = held.shape[1]
    cyc = lax.axis_index("cyc")
    base = cyc - lax.rem(cyc, near)
    me = (lax.axis_index("gx") * n_y + lax.axis_index("gy")) * near + lax.rem(cyc, near)

    def device(peer):
        plane = lax.div(peer, near)
        return (lax.div(plane, n_y), lax.rem(plane, n_y), base + lax.rem(peer, near))

    def chunk_at(ref, index):
        return ref.at[pl.ds(pl.multiple_of(index * chunk, 8), chunk)]

    def scatter(k):
        peer = lax.rem(me + k, n)
        return pltpu.make_async_remote_copy(
            src_ref=chunk_at(x_ref, peer), dst_ref=held.at[k],
            send_sem=send_a.at[k], recv_sem=recv_a.at[k],
            device_id=device(peer), device_id_type=MESH,
        )

    def gather(k):
        return pltpu.make_async_remote_copy(
            src_ref=chunk_at(o_ref, me), dst_ref=chunk_at(o_ref, me),
            send_sem=send_b.at[k], recv_sem=recv_b.at[k],
            device_id=device(lax.rem(me + k, n)), device_id_type=MESH,
        )

    def arrival(k):
        source = lax.rem(me - k + n, n)
        return pltpu.make_async_remote_copy(
            src_ref=chunk_at(o_ref, source), dst_ref=chunk_at(o_ref, source),
            send_sem=send_b.at[k], recv_sem=recv_b.at[k],
            device_id=device(source), device_id_type=MESH,
        )

    barrier = pltpu.get_barrier_semaphore()

    def loop(body):
        def step(k, carry):
            body(k)
            return carry

        lax.fori_loop(1, n, step, 0)

    loop(lambda k: pl.semaphore_signal(
        barrier, inc=1, device_id=device(lax.rem(me + k, n)), device_id_type=MESH))
    pl.semaphore_wait(barrier, n - 1)

    loop(lambda k: scatter(k).start())

    def added(k, total):
        scatter(k).wait_recv()
        return total + held[k]

    mine = pl.ds(pl.multiple_of(me * chunk, 8), chunk)
    o_ref[mine, :] = lax.fori_loop(1, n, added, x_ref[mine, :])
    loop(lambda k: gather(k).start())
    loop(lambda k: arrival(k).wait_recv())
    loop(lambda k: scatter(k).wait_send())
    loop(lambda k: gather(k).wait_send())


def group_size(near):
    return lax.axis_size("gx") * lax.axis_size("gy") * near


def padded_rows(near):
    n = group_size(near)
    chunk = -(-3 * RANK // (8 * n)) * 8
    return n * chunk


def summed(gram, near, ident):
    n = group_size(near)
    chunk = gram.shape[0] // n
    sizes = (lax.axis_size("gx"), lax.axis_size("gy"), near)
    return pl.pallas_call(
        functools.partial(sum_kernel, sizes),
        out_shape=jax.ShapeDtypeStruct(gram.shape, jnp.float32),
        in_specs=[pl.BlockSpec(memory_space=pltpu.VMEM)],
        out_specs=pl.BlockSpec(memory_space=pltpu.VMEM),
        scratch_shapes=[pltpu.VMEM((n, chunk, RANK), jnp.float32)]
        + [pltpu.SemaphoreType.DMA((n,))] * 4,
        compiler_params=pltpu.CompilerParams(
            collective_id=ident, has_side_effects=True, vmem_limit_bytes=VMEM_LIMIT
        ),
    )(gram)


def eliminate(work):
    parts = work.shape[1] // RANK
    for start in range(0, RANK, PANEL):
        rows = [
            [work[start + i : start + i + 1, p * RANK : (p + 1) * RANK] for p in range(parts)]
            for i in range(PANEL)
        ]
        block = [
            [
                jnp.broadcast_to(
                    work[start + i : start + i + 1, start + j : start + j + 1], (1, RANK)
                )
                for j in range(i + 1)
            ]
            for i in range(PANEL)
        ]
        for j in range(PANEL):
            scale = lax.rsqrt(block[j][j])
            rows[j] = [part * scale for part in rows[j]]
            column = {i: block[i][j] * scale for i in range(j + 1, PANEL)}
            for i in range(j + 1, PANEL):
                for k in range(j + 1, i + 1):
                    block[i][k] = block[i][k] - column[i] * column[k]
                rows[i] = [part - column[i] * top for part, top in zip(rows[i], rows[j])]
            for p in range(parts):
                work[start + j : start + j + 1, p * RANK : (p + 1) * RANK] = rows[j][p]
        after = start + PANEL
        if after < RANK:
            panel = work[start:after, :]
            work[after:, :] = work[after:, :] - contract(
                panel[:, after:RANK], panel, ((0,), (0,)), HIGHEST
            )


def vectors_kernel(gram_ref, v_ref, normed, work):
    width = 2 * RANK
    first = gram_ref[0:RANK]
    cross = gram_ref[RANK : 2 * RANK]
    last = gram_ref[2 * RANK : 3 * RANK]
    row = lax.broadcasted_iota(jnp.int32, (RANK, RANK), 0)
    col = lax.broadcasted_iota(jnp.int32, (RANK, RANK), 1)
    diagonal = jnp.where(row == col, first + last, 0.0)
    trace = jnp.sum(jnp.sum(diagonal, axis=0, keepdims=True), axis=1, keepdims=True)
    scale = 1.0 / (trace / width + 1e-06)
    normed[:RANK, :RANK] = first * scale
    normed[:RANK, RANK:] = cross * scale
    normed[RANK:, :RANK] = (cross * scale).T
    normed[RANK:, RANK:] = last * scale
    work[:, RANK:] = normed[:RANK, :] + normed[RANK:, :]

    def step(index, carry):
        @pl.when(index > 0)
        def _():
            work[:, RANK:] = contract(work[:, RANK:], normed[...], ((1,), (0,)), HIGHEST)

        moved = work[:, RANK:]
        work[:, :RANK] = contract(moved, moved, ((1,), (1,)), HIGHEST)
        eliminate(work)
        return carry

    lax.fori_loop(0, POWER, step, 0)
    v_ref[...] = work[:, RANK:]


def vectors_of(gram):
    return pl.pallas_call(
        vectors_kernel,
        out_shape=jax.ShapeDtypeStruct((RANK, 2 * RANK), jnp.float32),
        in_specs=[pl.BlockSpec(memory_space=pltpu.VMEM)],
        out_specs=pl.BlockSpec(memory_space=pltpu.VMEM),
        scratch_shapes=[
            pltpu.VMEM((2 * RANK, 2 * RANK), jnp.float32),
            pltpu.VMEM((RANK, 3 * RANK), jnp.float32),
        ],
        compiler_params=pltpu.CompilerParams(vmem_limit_bytes=VMEM_LIMIT),
    )(gram)


def on_device(displacement):
    groups = lax.axis_size("cyc")
    mine = lax.axis_index("cyc")
    low_bit = mine & 1
    side = mine >> 1
    parts, local_rows, local_cols, width = displacement.shape
    share = local_rows // groups
    halo = neighbours(displacement, "gx", 1) + neighbours(displacement, "gy", 2)
    field, gram = strain(displacement, halo, padded_rows(1))
    vectors = vectors_of(summed(gram, 1, 0))
    piece = contract(field.reshape(-1, width), vectors, ((1,), (1,)), HIGH)

    piece = piece.reshape(parts, groups // 2, 2, share * local_cols, RANK)
    own = jnp.where(low_bit == 0, piece[:, :, 0], piece[:, :, 1])
    other = exchanged(jnp.where(low_bit == 0, piece[:, :, 1], piece[:, :, 0]), 1)
    left = jnp.where(low_bit == 0, own, other)
    right = jnp.where(low_bit == 0, other, own)
    joined = jnp.concatenate([left, right], axis=3)
    kept = jnp.where(side == 0, joined[:, 0], joined[:, 1])
    arrived = exchanged(jnp.where(side == 0, joined[:, 1], joined[:, 0]), 2)
    gram = gram_of(left.reshape(-1, RANK), right.reshape(-1, RANK), padded_rows(2))
    vectors = vectors_of(summed(gram, 2, 1))
    far_vectors = exchanged(vectors, 2)

    kept = contract(kept.reshape(-1, 2 * RANK), vectors, ((1,), (1,)), HIGH)
    arrived = contract(arrived.reshape(-1, 2 * RANK), far_vectors, ((1,), (1,)), HIGH)
    left = jnp.where(side == 0, kept, arrived)
    right = jnp.where(side == 0, arrived, kept)
    gram = gram_of(left, right, padded_rows(4))
    vectors = vectors_of(summed(gram, 4, 2))
    basis = contract(vectors[:, :RANK], left, ((1,), (1,)), HIGH)
    basis = basis + contract(vectors[:, RANK:], right, ((1,), (1,)), HIGH)

    columns = RANK // groups
    basis = basis.reshape(groups, columns, -1)
    shares = [
        exchanged(lax.dynamic_index_in_dim(basis, mine ^ mask, 0, keepdims=False), mask)
        if mask
        else lax.dynamic_index_in_dim(basis, mine, 0, keepdims=False)
        for mask in range(groups)
    ]
    whole = jnp.stack(
        [
            lax.select_n(mine, *[shares[member ^ index] for index in range(groups)])
            for member in range(groups)
        ]
    )
    whole = whole.reshape(groups, columns, parts, share, local_cols)
    return whole.transpose(2, 0, 3, 4, 1).reshape(parts, local_rows, local_cols, columns)


def solution(mesh):
    return jax.shard_map(
        on_device,
        mesh=mesh,
        in_specs=(P(None, "gx", "gy", "cyc"),),
        out_specs=P(None, "gx", "gy", "cyc"),
        check_vma=False,
    )
```

```python
import functools

import jax
import jax.numpy as jnp
from jax import lax
from jax.experimental import pallas as pl
from jax.experimental.pallas import tpu as pltpu
from jax.sharding import PartitionSpec as P

RANK = 128
POWER = 3
PANEL = 16
MESH = pl.DeviceIdType.MESH
HIGH = lax.Precision.HIGH
HIGHEST = lax.Precision.HIGHEST
VMEM_LIMIT = 48 * 1024 * 1024


def halo_kernel(u_ref, top_ref, bottom_ref, xlo, xhi, ylo, yhi, send, recv):
    rows = u_ref.shape[1]
    sides = []
    for axis, low, high, first, last in (
        ("gx", xlo, xhi, u_ref.at[:, pl.ds(0, 1)], u_ref.at[:, pl.ds(rows - 1, 1)]),
        ("gy", ylo, yhi, top_ref, bottom_ref),
    ):
        at = lax.axis_index(axis)
        count = lax.axis_size(axis)
        has_low = at > 0
        has_high = at < count - 1
        below = {axis: jnp.maximum(at - 1, 0)}
        above = {axis: jnp.minimum(at + 1, count - 1)}
        sides.append((below, has_low, first, high, has_high))
        sides.append((above, has_high, last, low, has_low))

    barrier = pltpu.get_barrier_semaphore()
    for target, sends, *_ in sides:
        @pl.when(sends)
        def _():
            pl.semaphore_signal(barrier, inc=1, device_id=target, device_id_type=MESH)
    pl.semaphore_wait(barrier, sum(sends.astype(jnp.int32) for _, sends, *_ in sides))

    def copy(index):
        target, _, source, landing, _ = sides[index]
        return pltpu.make_async_remote_copy(
            src_ref=source, dst_ref=landing, send_sem=send.at[index], recv_sem=recv.at[index],
            device_id=target, device_id_type=MESH,
        )

    for index, (_, sends, _, landing, receives) in enumerate(sides):
        @pl.when(sends)
        def _():
            copy(index).start()

        @pl.when(jnp.logical_not(receives))
        def _():
            landing[...] = jnp.zeros_like(landing)
    for index, (_, sends, _, _, receives) in enumerate(sides):
        @pl.when(sends)
        def _():
            copy(index).wait_send()

        @pl.when(receives)
        def _():
            copy(index).wait_recv()


def halo_of(u):
    parts, rows, cols, width = u.shape
    top = u[:, :, 0].astype(jnp.float32).reshape(parts * rows, width)
    bottom = u[:, :, cols - 1].astype(jnp.float32).reshape(parts * rows, width)
    across = jax.ShapeDtypeStruct((parts, 1, cols, width), u.dtype)
    along = jax.ShapeDtypeStruct(top.shape, jnp.float32)
    vmem = pl.BlockSpec(memory_space=pltpu.VMEM)
    return pl.pallas_call(
        halo_kernel,
        out_shape=[across, across, along, along],
        in_specs=[pl.BlockSpec(memory_space=pl.ANY), vmem, vmem],
        out_specs=[vmem] * 4,
        scratch_shapes=[pltpu.SemaphoreType.DMA((4,))] * 2,
        compiler_params=pltpu.CompilerParams(
            collective_id=3, has_side_effects=True, vmem_limit_bytes=VMEM_LIMIT
        ),
    )(u, top, bottom)


def exchanged(value, mask):
    pairs = [(source, source ^ mask) for source in range(lax.axis_size("cyc"))]
    return lax.ppermute(value, "cyc", pairs)


def contract(left, right, dims, precision=None):
    return lax.dot_general(
        left, right, (dims, ((), ())), precision=precision, preferred_element_type=jnp.float32
    )


def upper_blocks(gram_ref, full):
    gram_ref[0:RANK] = full[:RANK, :RANK]
    gram_ref[RANK : 2 * RANK] = full[:RANK, RANK:]
    gram_ref[2 * RANK : 3 * RANK] = full[RANK:, RANK:]
    if gram_ref.shape[0] > 3 * RANK:
        gram_ref[3 * RANK :] = jnp.zeros((gram_ref.shape[0] - 3 * RANK, RANK), jnp.float32)


def split(value):
    high = value.astype(jnp.bfloat16)
    return high, (value - high.astype(jnp.float32)).astype(jnp.bfloat16)


def add_gram(main, cross, value):
    high, low = split(value)
    main[...] += contract(high, high, ((0,), (0,)))
    cross[...] += contract(high, low, ((0,), (0,)))


def strain_kernel(u_ref, xlo_ref, xhi_ref, ylo_ref, yhi_ref, f_ref, gram_ref, main, cross):
    i = pl.program_id(0)
    rows = u_ref.shape[1]
    cols = u_ref.shape[2]

    @pl.when(i == 0)
    def _():
        main[...] = jnp.zeros_like(main)
        cross[...] = jnp.zeros_like(cross)

    node = lax.broadcasted_iota(jnp.int32, (cols, u_ref.shape[3]), 0)

    def dx(part):
        before = u_ref[part, jnp.maximum(i - 1, 0)].astype(jnp.float32)
        after = u_ref[part, jnp.minimum(i + 1, rows - 1)].astype(jnp.float32)
        before = jnp.where(i == 0, xlo_ref[part, 0].astype(jnp.float32), before)
        after = jnp.where(i == rows - 1, xhi_ref[part, 0].astype(jnp.float32), after)
        return (after - before) * 0.5

    def dy(part):
        here = u_ref[part, i].astype(jnp.float32)
        before = pltpu.roll(here, 1, 0)
        after = pltpu.roll(here, cols - 1, 0)
        before = jnp.where(node == 0, ylo_ref[pl.ds(part * rows + i, 1), :], before)
        after = jnp.where(node == cols - 1, yhi_ref[pl.ds(part * rows + i, 1), :], after)
        return (after - before) * 0.5

    exx = dx(0)
    eyy = dy(1)
    exy = (dx(1) + dy(0)) * 0.5
    first = exx + eyy
    second = exx * eyy - exy * exy
    f_ref[0, 0] = first
    f_ref[1, 0] = second
    add_gram(main, cross, first)
    add_gram(main, cross, second)

    @pl.when(i == rows - 1)
    def _():
        upper_blocks(gram_ref, main[...] + cross[...] + cross[...].T)


def strain(u, halo, padded):
    parts, rows, cols, width = u.shape
    whole = [pl.BlockSpec(a.shape, lambda i, rank=a.ndim: (0,) * rank) for a in (u, *halo)]
    return pl.pallas_call(
        strain_kernel,
        grid=(rows,),
        in_specs=whole,
        out_specs=[
            pl.BlockSpec((parts, 1, cols, width), lambda i: (0, i, 0, 0)),
            pl.BlockSpec((padded, RANK), lambda i: (0, 0)),
        ],
        out_shape=[
            jax.ShapeDtypeStruct((parts, rows, cols, width), jnp.float32),
            jax.ShapeDtypeStruct((padded, RANK), jnp.float32),
        ],
        scratch_shapes=[pltpu.VMEM((width, width), jnp.float32)] * 2,
        compiler_params=pltpu.CompilerParams(vmem_limit_bytes=VMEM_LIMIT),
    )(u, *halo)


def cross_kernel(left_ref, right_ref, gram_ref):
    step = pl.program_id(0)

    @pl.when(step == 0)
    def _():
        gram_ref[...] = jnp.zeros_like(gram_ref)

    left_high, left_low = split(left_ref[...])
    right_high, right_low = split(right_ref[...])
    rows = ((0,), (0,))
    gram_ref[:RANK] += (
        contract(left_high, right_high, rows)
        + contract(left_high, right_low, rows)
        + contract(left_low, right_high, rows)
    )


def cross_of(left, right, padded):
    rows = left.shape[0]
    tile = 512 if rows % 512 == 0 else rows
    spec = pl.BlockSpec((tile, RANK), lambda i: (i, 0))
    return pl.pallas_call(
        cross_kernel,
        grid=(rows // tile,),
        in_specs=[spec, spec],
        out_specs=pl.BlockSpec((padded, RANK), lambda i: (0, 0)),
        out_shape=jax.ShapeDtypeStruct((padded, RANK), jnp.float32),
        compiler_params=pltpu.CompilerParams(vmem_limit_bytes=VMEM_LIMIT),
    )(left, right)


def sum_kernel(sizes, x_ref, o_ref, held, send_a, recv_a, send_b, recv_b):
    n_x, n_y, near = sizes
    n = n_x * n_y * near
    chunk = held.shape[1]
    cyc = lax.axis_index("cyc")
    base = cyc - lax.rem(cyc, near)
    me = (lax.axis_index("gx") * n_y + lax.axis_index("gy")) * near + lax.rem(cyc, near)

    def device(peer):
        plane = lax.div(peer, near)
        return (lax.div(plane, n_y), lax.rem(plane, n_y), base + lax.rem(peer, near))

    def chunk_at(ref, index):
        return ref.at[pl.ds(pl.multiple_of(index * chunk, 8), chunk)]

    def scatter(k):
        peer = lax.rem(me + k, n)
        return pltpu.make_async_remote_copy(
            src_ref=chunk_at(x_ref, peer), dst_ref=held.at[k],
            send_sem=send_a.at[k], recv_sem=recv_a.at[k],
            device_id=device(peer), device_id_type=MESH,
        )

    def gather(k):
        return pltpu.make_async_remote_copy(
            src_ref=chunk_at(o_ref, me), dst_ref=chunk_at(o_ref, me),
            send_sem=send_b.at[k], recv_sem=recv_b.at[k],
            device_id=device(lax.rem(me + k, n)), device_id_type=MESH,
        )

    def arrival(k):
        source = lax.rem(me - k + n, n)
        return pltpu.make_async_remote_copy(
            src_ref=chunk_at(o_ref, source), dst_ref=chunk_at(o_ref, source),
            send_sem=send_b.at[k], recv_sem=recv_b.at[k],
            device_id=device(source), device_id_type=MESH,
        )

    barrier = pltpu.get_barrier_semaphore()

    def loop(body):
        def step(k, carry):
            body(k)
            return carry

        lax.fori_loop(1, n, step, 0)

    loop(lambda k: pl.semaphore_signal(
        barrier, inc=1, device_id=device(lax.rem(me + k, n)), device_id_type=MESH))
    pl.semaphore_wait(barrier, n - 1)

    loop(lambda k: scatter(k).start())

    def added(k, total):
        scatter(k).wait_recv()
        return total + held[k]

    mine = pl.ds(pl.multiple_of(me * chunk, 8), chunk)
    o_ref[mine, :] = lax.fori_loop(1, n, added, x_ref[mine, :])
    loop(lambda k: gather(k).start())
    loop(lambda k: arrival(k).wait_recv())
    loop(lambda k: scatter(k).wait_send())
    loop(lambda k: gather(k).wait_send())


def group_size(near):
    return lax.axis_size("gx") * lax.axis_size("gy") * near


def padded_rows(near, blocks):
    n = group_size(near)
    chunk = -(-blocks * RANK // (8 * n)) * 8
    return n * chunk


def summed(gram, near, ident):
    n = group_size(near)
    chunk = gram.shape[0] // n
    sizes = (lax.axis_size("gx"), lax.axis_size("gy"), near)
    return pl.pallas_call(
        functools.partial(sum_kernel, sizes),
        out_shape=jax.ShapeDtypeStruct(gram.shape, jnp.float32),
        in_specs=[pl.BlockSpec(memory_space=pltpu.VMEM)],
        out_specs=pl.BlockSpec(memory_space=pltpu.VMEM),
        scratch_shapes=[pltpu.VMEM((n, chunk, RANK), jnp.float32)]
        + [pltpu.SemaphoreType.DMA((n,))] * 4,
        compiler_params=pltpu.CompilerParams(
            collective_id=ident, has_side_effects=True, vmem_limit_bytes=VMEM_LIMIT
        ),
    )(gram)


def eliminate(work):
    def row_of(value, index):
        return value[index : index + 1, :]

    for start in range(0, RANK, PANEL):
        after = start + PANEL
        rest = work[start:after, :]
        columns = [
            jnp.broadcast_to(work[start:after, start + k : start + k + 1], (PANEL, RANK))
            for k in range(PANEL)
        ]
        wide = lambda value: jnp.concatenate([value] * (rest.shape[1] // RANK), axis=1)
        for j in range(0, PANEL, 2):
            one = row_of(columns[j], j)
            mixed = row_of(columns[j], j + 1)
            two = row_of(columns[j + 1], j + 1)
            root = lax.rsqrt(one)
            second = lax.rsqrt(one * two - mixed * mixed) * (one * root)
            lower = mixed * root
            left = columns[j] * root
            right = (columns[j + 1] - left * lower) * second
            top = row_of(rest, j) * wide(root)
            bottom = (row_of(rest, j + 1) - top * wide(lower)) * wide(second)
            work[start + j : start + j + 1, :] = top
            work[start + j + 1 : start + j + 2, :] = bottom
            if j + 2 < PANEL:
                for k in range(j + 2, PANEL):
                    columns[k] = columns[k] - (
                        left * row_of(left, k) + right * row_of(right, k)
                    )
                rest = rest - (wide(left) * top + wide(right) * bottom)
        if after < RANK:
            panel = work[start:after, :]
            work[after:, :] = work[after:, :] - contract(
                panel[:, after:RANK], panel, ((0,), (0,)), HIGHEST
            )


def vectors_kernel(first_ref, cross_ref, last_ref, v_ref, own_ref, normed, work):
    width = 2 * RANK
    first = first_ref[...]
    cross = cross_ref[...]
    last = last_ref[...]
    row = lax.broadcasted_iota(jnp.int32, (RANK, RANK), 0)
    col = lax.broadcasted_iota(jnp.int32, (RANK, RANK), 1)
    diagonal = jnp.where(row == col, first + last, 0.0)
    trace = jnp.sum(jnp.sum(diagonal, axis=0, keepdims=True), axis=1, keepdims=True)
    level = trace / width + 1e-06
    scale = 1.0 / level
    normed[:RANK, :RANK] = first * scale
    normed[:RANK, RANK:] = cross * scale
    normed[RANK:, :RANK] = (cross * scale).T
    normed[RANK:, RANK:] = last * scale
    work[:, RANK:] = normed[:RANK, :] + normed[RANK:, :]

    def step(index, carry):
        @pl.when(index > 0)
        def _():
            work[:, RANK:] = contract(work[:, RANK:], normed[...], ((1,), (0,)), HIGHEST)

        moved = work[:, RANK:]
        gram = contract(moved, moved, ((1,), (1,)), HIGHEST)
        kept = jnp.where(row == col, gram, 0.0)
        down = lax.rsqrt(jnp.sum(kept, axis=1, keepdims=True))
        along = lax.rsqrt(jnp.sum(kept, axis=0, keepdims=True))
        work[:, :RANK] = gram * down * along
        work[:, RANK:] = moved * down
        eliminate(work)
        return carry

    lax.fori_loop(0, POWER, step, 0)
    vectors = work[:, RANK:]
    v_ref[...] = vectors
    moved = contract(vectors, normed[...], ((1,), (0,)), HIGHEST)
    own_ref[...] = contract(moved, vectors, ((1,), (1,)), HIGHEST) * level


def vectors_of(*blocks):
    tile = (RANK, RANK)
    return pl.pallas_call(
        vectors_kernel,
        grid=(1,),
        out_shape=[
            jax.ShapeDtypeStruct((RANK, 2 * RANK), jnp.float32),
            jax.ShapeDtypeStruct(tile, jnp.float32),
        ],
        in_specs=[pl.BlockSpec(tile, lambda i, at=at: (at, 0)) for _, at in blocks],
        out_specs=[
            pl.BlockSpec((RANK, 2 * RANK), lambda i: (0, 0)),
            pl.BlockSpec(tile, lambda i: (0, 0)),
        ],
        scratch_shapes=[
            pltpu.VMEM((2 * RANK, 2 * RANK), jnp.float32),
            pltpu.VMEM((RANK, 3 * RANK), jnp.float32),
        ],
        compiler_params=pltpu.CompilerParams(vmem_limit_bytes=VMEM_LIMIT),
    )(*[array for array, _ in blocks])


def on_device(displacement):
    groups = lax.axis_size("cyc")
    mine = lax.axis_index("cyc")
    low_bit = mine & 1
    side = mine >> 1
    parts, local_rows, local_cols, width = displacement.shape
    share = local_rows // groups
    field, gram = strain(displacement, halo_of(displacement), padded_rows(1, 3))
    gram = summed(gram, 1, 0)
    vectors, own_gram = vectors_of((gram, 0), (gram, 1), (gram, 2))
    other_gram = exchanged(own_gram, 1)
    piece = contract(field.reshape(-1, width), vectors, ((1,), (1,)), HIGH)

    piece = piece.reshape(parts, groups // 2, 2, share * local_cols, RANK)
    own = jnp.where(low_bit == 0, piece[:, :, 0], piece[:, :, 1])
    other = exchanged(jnp.where(low_bit == 0, piece[:, :, 1], piece[:, :, 0]), 1)
    left = jnp.where(low_bit == 0, own, other)
    right = jnp.where(low_bit == 0, other, own)
    joined = jnp.concatenate([left, right], axis=3)
    kept = jnp.where(side == 0, joined[:, 0], joined[:, 1])
    arrived = exchanged(jnp.where(side == 0, joined[:, 1], joined[:, 0]), 2)
    cross = cross_of(left.reshape(-1, RANK), right.reshape(-1, RANK), padded_rows(2, 1))
    first = jnp.where(low_bit == 0, own_gram, other_gram)
    last = jnp.where(low_bit == 0, other_gram, own_gram)
    vectors, own_gram = vectors_of((first, 0), (summed(cross, 2, 1), 0), (last, 0))
    far = exchanged(jnp.concatenate([vectors, own_gram], axis=1), 2)
    far_vectors, far_gram = far[:, : 2 * RANK], far[:, 2 * RANK :]

    kept = contract(kept.reshape(-1, 2 * RANK), vectors, ((1,), (1,)), HIGH)
    arrived = contract(arrived.reshape(-1, 2 * RANK), far_vectors, ((1,), (1,)), HIGH)
    left = jnp.where(side == 0, kept, arrived)
    right = jnp.where(side == 0, arrived, kept)
    cross = cross_of(left, right, padded_rows(4, 1))
    first = jnp.where(side == 0, own_gram, far_gram)
    last = jnp.where(side == 0, far_gram, own_gram)
    vectors, _ = vectors_of((first, 0), (summed(cross, 4, 2), 0), (last, 0))
    basis = contract(vectors[:, :RANK], left, ((1,), (1,)), HIGH)
    basis = basis + contract(vectors[:, RANK:], right, ((1,), (1,)), HIGH)

    columns = RANK // groups
    basis = basis.reshape(groups, columns, -1)
    shares = [
        exchanged(lax.dynamic_index_in_dim(basis, mine ^ mask, 0, keepdims=False), mask)
        if mask
        else lax.dynamic_index_in_dim(basis, mine, 0, keepdims=False)
        for mask in range(groups)
    ]
    whole = jnp.stack(
        [
            lax.select_n(mine, *[shares[member ^ index] for index in range(groups)])
            for member in range(groups)
        ]
    )
    whole = whole.reshape(groups, columns, parts, share, local_cols)
    return whole.transpose(2, 0, 3, 4, 1).reshape(parts, local_rows, local_cols, columns)


def solution(mesh):
    return jax.shard_map(
        on_device,
        mesh=mesh,
        in_specs=(P(None, "gx", "gy", "cyc"),),
        out_specs=P(None, "gx", "gy", "cyc"),
        check_vma=False,
    )
```
